256 devices in a mesh: seq: 16 (over z, core), wt: 16 (over x, y).
Axes of the slice: x: 4, y: 4, z: 8, core: 2. Of those that a mesh axis runs over, the one named last changes fastest.
Arguments:
- queries: bfloat16 [8192, 8192], P('seq', 'wt'), may hold values from -6 to 6
- keys_in: bfloat16 [8192, 8192], P('seq', 'wt'), may hold values from -6 to 6
- values_in: bfloat16 [8192, 8192], P('seq', 'wt'), may hold values from -6 to 6
- stream: bfloat16 [8192, 8192], P('seq', 'wt')
- attn_gain: float32 [8192], P('wt'), may hold values from 0.1 to 1.9
- mlp_gain: float32 [8192], replicated, may hold values from 0.1 to 1.9
- up_index: int32 [128, 16], P('wt'), may hold values from 0 to 63, all different within a row
- up_blocks: bfloat16 [128, 16, 128, 128], P('wt'), may hold values from -0.125 to 0.125
- down_index: int32 [128, 16], P('wt'), may hold values from 0 to 63, all different within a row
- down_blocks: bfloat16 [128, 16, 128, 128], P('wt'), may hold values from -0.09375 to 0.09375
Outputs:
- result: bfloat16 [8192, 8192], P('seq', 'wt')
The draws below stay inside these ranges and needn't reach their ends.
Inputs may be any that keep to these rules, and one draw needn't show every extreme that they name: `up_index`: each row names 16 different feature blocks, and every feature block is named by some row. `down_index`: each row names 16 different output blocks, and every output block is named by some row.
All inputs are finite; a program needn't handle non-finite values.
Results may differ from the reference program's by a relative error of at most 0.013.
Values may be sent and summed in bfloat16 or wider, within the bound.
No kernel may reach another device: no remote copies, remote signals or barrier semaphores. Data moves between devices by JAX's collectives and lax.ppermute only.
A program may use at most 128 MiB of HBM per device.

```python
import math
import jax
import jax.numpy as jnp
from jax import lax

HEADS = 64
HEAD = 128
D = 8192
FF = 16384
BLK = 128
KEEP_IN = 16
KEEP_OUT = 16
L_DEV = 512
TOKENS = 8192
N_WT = 16


def draw_stream(key, part):
    key_cols, key_rows, key_base = jax.random.split(jax.random.fold_in(key, 17), 3)
    ramp = jnp.exp(math.log(3.0) * jnp.arange(D, dtype=jnp.float32) / D)
    jitter = jnp.exp(jax.random.uniform(key_cols, (1, D), minval=math.log(0.6), maxval=math.log(1.6)))
    cols = 0.5 * ramp[None, :] * jitter
    rows = jnp.exp(jax.random.uniform(key_rows, (TOKENS, 1), minval=math.log(0.6), maxval=math.log(1.6)))
    base = jnp.clip(jax.random.normal(key_base, (TOKENS, D)), -4.0, 4.0)
    return (base * rows * cols).astype(jnp.bfloat16)


def shard_levels(rng, extent, shards, smallest, largest):
    level, own = 1.0, jax.random.fold_in(rng, 6)
    for dim, blocks in shards:
        heights = jnp.exp(jax.random.uniform(jax.random.fold_in(own, dim), (blocks,), jnp.float32, smallest / len(shards), largest / len(shards)))
        level = level * jnp.repeat(heights, extent[dim] // blocks).reshape([-1 if axis == dim else 1 for axis in range(len(extent))])
    return level


def different_ones(rng, rows, amount, top, lift):
    ranking = jax.random.permutation(jax.random.fold_in(rng, 1), amount)
    pull = ranking
    for power in range(3):
        pull = pull * pull // amount
    pull = pull * lift // amount
    tickets = jax.random.randint(jax.random.fold_in(rng, 2), (rows, amount), 0, 4096) + pull
    fixed_rows = jax.random.permutation(jax.random.fold_in(rng, 3), rows)[jnp.arange(amount) % rows]
    tickets = jnp.where(jnp.arange(rows)[:, None] == fixed_rows[None, :], 1 << 14, tickets)
    merit = tickets * amount + jnp.arange(amount)
    return lax.top_k(merit.astype(jnp.int32), top)[1].astype(jnp.int32)


def centred(key, shape, scale, most, pieces=(), kind=jnp.bfloat16):
    level = shard_levels(key, shape, pieces, -0.22, 0.18) if pieces else 1.0
    entries = jax.random.normal(key, shape, jnp.float32) * scale * level
    return jnp.minimum(jnp.maximum(entries, -most), most).astype(kind)


def setup_inputs(seed: int = 0) -> dict:
    key_list = jax.random.split(jax.random.key(seed), 11)
    queries = centred(key_list[0], (TOKENS, D), 1.0, 6.0, ((0, 16), (1, 16)))
    keys_in = centred(key_list[1], (TOKENS, D), 1.0, 6.0, ((0, 16), (1, 16)))
    values_in = centred(key_list[2], (TOKENS, D), 1.0, 6.0, ((0, 16), (1, 16)))
    stream = draw_stream(jax.random.fold_in(key_list[10], 71), 0)
    attn_gain = jnp.clip(1.0 + 0.18 * jax.random.normal(key_list[4], (D,), jnp.float32), 0.1, 1.9)
    mlp_gain = jnp.clip(1.0 + 0.18 * jax.random.normal(key_list[5], (D,), jnp.float32), 0.1, 1.9)
    up_index = different_ones(key_list[6], (FF // BLK), D // BLK, KEEP_IN, 0)
    up_blocks = centred(key_list[7], (FF // BLK, KEEP_IN, BLK, BLK), (KEEP_IN * BLK) ** -0.5, 0.125, ((0, 16),))
    down_index = different_ones(key_list[8], (FF // BLK), D // BLK, KEEP_OUT, 0)
    down_blocks = centred(key_list[9], (FF // BLK, KEEP_OUT, BLK, BLK), (FF * KEEP_OUT // (D // BLK)) ** -0.5, 0.09375, ((0, 16),))
    return {"queries": queries, "keys_in": keys_in, "values_in": values_in, "stream": stream, "attn_gain": attn_gain, "mlp_gain": mlp_gain, "up_index": up_index, "up_blocks": up_blocks, "down_index": down_index, "down_blocks": down_blocks}


def feature_map(a):
    return (jax.nn.elu(a.astype(jnp.float32)) + 1.0).astype(jnp.bfloat16)

def reference(queries, keys_in, values_in, stream, attn_gain, mlp_gain, up_index, up_blocks, down_index, down_blocks):
    blocks = TOKENS // L_DEV
    fq = feature_map(queries).reshape(blocks, L_DEV, HEADS, HEAD)
    fk = feature_map(keys_in).reshape(blocks, L_DEV, HEADS, HEAD)
    vals = values_in.reshape(blocks, L_DEV, HEADS, HEAD)
    causal = jnp.tril(jnp.ones((L_DEV, L_DEV), dtype=bool))

    def advance(state, piece):
        bq, bk, bv = piece
        scores = jnp.einsum('thd,shd->hts', bq.astype(jnp.float32), bk.astype(jnp.float32))
        scores = jnp.where(causal[None], scores, 0.0).astype(jnp.bfloat16)
        intra = jnp.einsum('hts,shd->thd', scores.astype(jnp.float32), bv.astype(jnp.float32))
        inter = jnp.einsum('thd,hde->the', bq.astype(jnp.float32), state, precision=lax.Precision.HIGHEST)
        grown = state + jnp.einsum('shd,she->hde', bk.astype(jnp.float32), bv.astype(jnp.float32))
        return (grown, intra + inter)
    start = jnp.zeros((HEADS, HEAD, HEAD), jnp.float32)
    _, raw = lax.scan(advance, start, (fq, fk, vals))
    raw = raw.reshape(TOKENS, HEADS, HEAD)
    normal_raw = raw * lax.rsqrt(lax.optimization_barrier(jnp.mean(raw * raw, axis=-1, keepdims=True)) + 1e-06)
    attn = normal_raw.reshape(TOKENS, D) * attn_gain.astype(jnp.float32)
    mid = (stream.astype(jnp.float32) + attn).astype(jnp.bfloat16)
    up_float = up_blocks.astype(jnp.float32)
    down_float = down_blocks.astype(jnp.float32)
    groups = N_WT
    per_group = FF // BLK // groups
    group_down = down_index.reshape(groups, per_group * KEEP_OUT).astype(jnp.int32)

    def feed(rows):
        rows_f = rows.astype(jnp.float32)
        scale = lax.rsqrt(lax.optimization_barrier(jnp.mean(rows_f * rows_f, axis=-1, keepdims=True)) + 1e-06)
        normed = (rows_f * scale * mlp_gain.astype(jnp.float32)).astype(jnp.bfloat16)
        tiles = normed.reshape(L_DEV, D // BLK, BLK)
        picks = tiles[:, up_index.astype(jnp.int32)]
        upper = jnp.einsum('lckd,ckde->lce', picks.astype(jnp.float32), up_float)
        act = jax.nn.silu(upper).astype(jnp.bfloat16)
        parts = jnp.einsum('lrd,rkde->rkle', act.astype(jnp.float32), down_float)
        parts = parts.reshape(groups, per_group * KEEP_OUT, L_DEV, BLK)

        def one_group(total, item):
            piece, index_row = item
            partial_sum = jax.ops.segment_sum(piece, index_row, num_segments=D // BLK)
            return (total + partial_sum.astype(jnp.bfloat16).astype(jnp.float32), None)
        zero_sum = jnp.zeros((D // BLK, L_DEV, BLK), jnp.float32)
        summed, _ = lax.scan(one_group, zero_sum, (parts, group_down))
        down = jnp.transpose(summed, (1, 0, 2)).reshape(L_DEV, D)
        return (rows_f + down).astype(jnp.bfloat16)
    outcome = lax.map(feed, mid.reshape(blocks, L_DEV, D))
    return outcome.reshape(TOKENS, D)
```

```python
import functools

import jax
import jax.numpy as jnp
from jax import lax
from jax.experimental import pallas as pl
from jax.experimental.pallas import tpu as pltpu
from jax.sharding import PartitionSpec as P

HEAD = 128
BLK = 128
SIDE = 4
F32 = jnp.float32
BF16 = jnp.bfloat16
VMEM = pl.BlockSpec(memory_space=pltpu.VMEM)
SMEM = pl.BlockSpec(memory_space=pltpu.SMEM)
ANY = pl.BlockSpec(memory_space=pl.ANY)


def feature(a):
    a = a.astype(F32)
    return jnp.where(a > 0, a + 1.0, jnp.exp(jnp.minimum(a, 0.0))).astype(BF16)


def dot(a, b):
    return jnp.dot(a, b, preferred_element_type=F32)


def dot_nt(a, b):
    return lax.dot_general(a, b, (((1,), (1,)), ((), ())), preferred_element_type=F32)


def dot_tn(a, b):
    return lax.dot_general(a, b, (((0,), (0,)), ((), ())), preferred_element_type=F32)


def state_kernel(k_ref, v_ref, out_ref):
    for h in range(4):
        cols = slice(h * HEAD, (h + 1) * HEAD)
        out_ref[h] = dot_tn(feature(k_ref[:, cols]), v_ref[:, cols]).astype(BF16)


def intra_kernel(q_ref, k_ref, v_ref, out_ref):
    half = 256
    row = lax.broadcasted_iota(jnp.int32, (half, half), 0)
    col = lax.broadcasted_iota(jnp.int32, (half, half), 1)
    keep = col <= row
    for h in range(4):
        cols = slice(h * HEAD, (h + 1) * HEAD)
        fq = feature(q_ref[:, cols])
        fk = feature(k_ref[:, cols])
        v = v_ref[:, cols]
        top = jnp.where(keep, dot_nt(fq[:half], fk[:half]), 0.0).astype(BF16)
        out_ref[h, :half] = dot(top, v[:half])
        left = dot_nt(fq[half:], fk[:half]).astype(BF16)
        right = jnp.where(keep, dot_nt(fq[half:], fk[half:]), 0.0).astype(BF16)
        out_ref[h, half:] = dot(left, v[:half]) + dot(right, v[half:])


def mid_kernel(q_ref, state_ref, intra_ref, stream_ref, gain_ref, a_ref, b_ref):
    for h in range(4):
        cols = slice(h * HEAD, (h + 1) * HEAD)
        fq = feature(q_ref[:, cols])
        state = state_ref[h]
        high = state.astype(BF16)
        low = (state - high.astype(F32)).astype(BF16)
        raw = intra_ref[h] + dot(fq, high) + dot(fq, low)
        scale = lax.rsqrt(jnp.mean(raw * raw, axis=-1, keepdims=True) + 1e-06)
        attn = raw * scale * gain_ref[:, cols]
        mid = (stream_ref[:, cols].astype(F32) + attn).astype(BF16)
        for t in range(2):
            a_ref[t, h] = mid[t * 128 : (t + 1) * 128]
            b_ref[t, h] = mid[256 + t * 128 : 256 + (t + 1) * 128]


def ffn_kernel(places_in, places_out, up_index, down_index, gain_ref, *refs):
    pieces = refs[:8]
    up_hbm, down_hbm = refs[8:10]
    outs = refs[10:18]
    x, up_w, down_w, acc, stage, in_sem, up_sem, down_sem, out_sem = refs[18:]
    n_hidden = up_w.shape[0]
    kept = up_w.shape[1]

    def piece_copy(i, t):
        place = places_in[i]
        return pltpu.make_async_copy(
            pieces[(i // 4) * 2 + t].at[i % 4],
            x.at[pl.ds(place * 4, 4), pl.ds(t * 128, 128), :],
            in_sem.at[i, t],
        )

    def up_copy(c):
        return pltpu.make_async_copy(up_hbm.at[c], up_w.at[c], up_sem.at[c])

    def down_copy(c):
        return pltpu.make_async_copy(down_hbm.at[c], down_w.at[c], down_sem.at[c])

    for i in range(16):
        for t in range(2):
            piece_copy(i, t).start()
    for c in range(n_hidden):
        up_copy(c).start()
    for c in range(n_hidden):
        down_copy(c).start()

    @pl.loop(0, 64)
    def _(j):
        acc[j] = jnp.zeros((256, 128), F32)

    squares = jnp.zeros((256, 128), F32)
    for i in range(16):
        piece_copy(i, 0).wait()
        piece_copy(i, 1).wait()
        place = places_in[i]
        for b in range(4):
            block = place * 4 + b
            value = x[block].astype(F32)
            squares = squares + value * value
            x[block] = (value * gain_ref[pl.ds(block, 1), :]).astype(BF16)
    mean = jnp.sum(squares, axis=-1, keepdims=True) * (1.0 / (64 * 128))
    scale = lax.rsqrt(mean + 1e-06)

    @pl.loop(0, n_hidden)
    def _(c):
        up_copy(c).wait()
        picked = jnp.concatenate([x[up_index[c, k]] for k in range(kept)], axis=1)
        upper = dot(picked, up_w[c].reshape(kept * BLK, BLK)) * scale
        act = (upper / (1.0 + jnp.exp(-upper))).astype(BF16)
        down_copy(c).wait()
        for k in range(0, kept, 2):
            pair = jnp.concatenate([down_w[c, k], down_w[c, k + 1]], axis=1)
            part = dot(act, pair)
            acc[down_index[c, k]] += part[:, :BLK]
            acc[down_index[c, k + 1]] += part[:, BLK:]

    def out_copy(i, t):
        return pltpu.make_async_copy(
            stage.at[pl.ds(i * 4, 4), pl.ds(t * 128, 128), :],
            outs[(i // 4) * 2 + t].at[i % 4],
            out_sem.at[i, t],
        )

    for i in range(16):
        place = places_out[i]
        for b in range(4):
            stage[i * 4 + b] = acc[place * 4 + b].astype(BF16)
        for t in range(2):
            out_copy(i, t).start()
    for i in range(16):
        for t in range(2):
            out_copy(i, t).wait()


def ffn(pieces, places_in, places_out, up_index, down_index, gain, up_blocks, down_blocks):
    n_hidden, kept = up_index.shape
    piece = jax.ShapeDtypeStruct((4, 4, 128, 128), BF16)
    return pl.pallas_call(
        ffn_kernel,
        out_shape=[piece] * 8,
        in_specs=[SMEM] * 4 + [VMEM] + [ANY] * 10,
        out_specs=[ANY] * 8,
        scratch_shapes=[
            pltpu.VMEM((64, 256, 128), BF16),
            pltpu.VMEM((n_hidden, kept, BLK, BLK), BF16),
            pltpu.VMEM((n_hidden, kept, BLK, BLK), BF16),
            pltpu.VMEM((64, 256, 128), F32),
            pltpu.VMEM((64, 256, 128), BF16),
            pltpu.SemaphoreType.DMA((16, 2)),
            pltpu.SemaphoreType.DMA((n_hidden,)),
            pltpu.SemaphoreType.DMA((n_hidden,)),
            pltpu.SemaphoreType.DMA((16, 2)),
        ],
        compiler_params=pltpu.CompilerParams(vmem_limit_bytes=44 * 2**20),
        cost_estimate=pl.CostEstimate(
            flops=4 * 256 * n_hidden * kept * BLK * BLK, bytes_accessed=17 * 2**20, transcendentals=256 * 1024
        ),
        name="feed_forward",
    )(places_in, places_out, up_index, down_index, gain, *pieces, up_blocks, down_blocks)


def final_kernel(*refs):
    out_ref = refs[-1]
    for half in range(2):
        parts = refs[half * 5 : half * 5 + 5]
        for t in range(2):
            rows = slice(half * 256 + t * 128, half * 256 + (t + 1) * 128)
            for b in range(4):
                down = sum((p[t, b].astype(F32) for p in parts[2:]), parts[1][t, b].astype(F32))
                total = parts[0][t, b].astype(F32) + down
                out_ref[rows, b * BLK : (b + 1) * BLK] = total.astype(BF16)


def torus_shift(x, axis, step):
    step_x, step_y = (step, 0) if axis == 0 else (0, step)
    pairs = [
        (a * SIDE + b, ((a + step_x) % SIDE) * SIDE + (b + step_y) % SIDE) for a in range(SIDE) for b in range(SIDE)
    ]
    return lax.ppermute(x, "wt", pairs)


def ring_all(x, axis):
    ahead, back, far = torus_shift(x, axis, 1), torus_shift(x, axis, -1), torus_shift(x, axis, 2)
    return [x, ahead, far, back]


def ring_rows(first, second, axis):
    first_1 = torus_shift(first, axis, 1)
    second_3 = torus_shift(second, axis, -1)
    second_1 = torus_shift(second, axis, 1)
    first_3 = torus_shift(first, axis, -1)
    first_2 = torus_shift(first_1, axis, 1)
    second_2 = torus_shift(second_3, axis, -1)
    return [first, second, first_1, second_1, first_2, second_2, first_3, second_3]


def gather_half(mid, inner, outer):
    near = ring_all(mid, inner)
    first = jnp.stack([n[0] for n in near])
    second = jnp.stack([n[1] for n in near])
    return ring_rows(first, second, outer)


def added(*terms):
    total = terms[0].astype(F32)
    for t in terms[1:]:
        total = total + t.astype(F32)
    return total.astype(BF16)


def scatter_half(p, inner, outer):
    a = torus_shift(p[4], outer, 1)
    b = torus_shift(p[5], outer, -1)
    c = torus_shift(p[3], outer, 1)
    d = torus_shift(p[6], outer, -1)
    a2 = torus_shift(added(a, p[2]), outer, 1)
    b2 = torus_shift(added(b, p[7]), outer, -1)
    rows = [jnp.stack([added(p[0][r], a2[r], d[r]), added(p[1][r], b2[r], c[r])]) for r in range(4)]
    from_1 = torus_shift(rows[1], inner, 1)
    from_3 = torus_shift(rows[3], inner, -1)
    from_2 = torus_shift(rows[2], inner, 2)
    return [rows[0], from_1, from_2, from_3]


def states_before(own, seq_size):
    core = lax.axis_index("seq") % 2
    other = lax.ppermute(own, "seq", [(s, s ^ 1) for s in range(seq_size)])

    def later(x, places):
        return lax.ppermute(x, "seq", [(s, s + 2 * places) for s in range(seq_size) if s + 2 * places < seq_size])

    both = own.astype(F32) + other.astype(F32)
    pair = jnp.where(core == 0, both[:2], both[2:]).astype(BF16)
    near = later(pair, 1).astype(F32) + later(pair, 2).astype(F32)
    window = (near + pair.astype(F32)).astype(BF16)
    before = near + later(window, 3).astype(F32) + later(window, 6).astype(F32)
    rest = lax.ppermute(before.astype(BF16), "seq", [(s, s ^ 1) for s in range(seq_size)]).astype(F32)
    whole = jnp.where(core == 0, jnp.concatenate([before, rest]), jnp.concatenate([rest, before]))
    return whole + jnp.where(core == 0, 0.0, other.astype(F32))


def per_device(seq_size, queries, keys_in, values_in, stream, attn_gain, mlp_gain, up_index, up_blocks, down_index, down_blocks):
    own = pl.pallas_call(
        state_kernel,
        out_shape=jax.ShapeDtypeStruct((4, HEAD, HEAD), BF16),
        in_specs=[VMEM] * 2,
        out_specs=VMEM,
        name="states",
    )(keys_in, values_in)
    intra = pl.pallas_call(
        intra_kernel,
        out_shape=jax.ShapeDtypeStruct((4, 512, HEAD), F32),
        in_specs=[VMEM] * 3,
        out_specs=VMEM,
        cost_estimate=pl.CostEstimate(flops=2**30, bytes_accessed=3 * 2**20, transcendentals=2**19),
        name="within_block",
    )(queries, keys_in, values_in)
    before = states_before(own, seq_size)
    half = jax.ShapeDtypeStruct((2, 4, 128, 128), BF16)
    mid_a, mid_b = pl.pallas_call(
        mid_kernel,
        out_shape=[half, half],
        in_specs=[VMEM] * 5,
        out_specs=[VMEM] * 2,
        name="mid",
    )(queries, before, intra, stream, attn_gain.reshape(1, -1))

    place = lax.axis_index("wt")
    at_x, at_y = place // SIDE, place % SIDE
    outer, inner = jnp.arange(16, dtype=jnp.int32) // 4, jnp.arange(16, dtype=jnp.int32) % 4

    def where(step_x, step_y):
        return ((at_x + step_x + SIDE) % SIDE) * SIDE + (at_y + step_y + SIDE) % SIDE

    gain = mlp_gain.reshape(64, BLK)
    local = (up_index, down_index, gain, up_blocks, down_blocks)
    all_a = gather_half(mid_a, 0, 1)
    all_b = gather_half(mid_b, 1, 0)
    sums_a = ffn(all_a, where(-inner, -outer), where(inner, outer), *local)
    sums_b = ffn(all_b, where(-outer, -inner), where(outer, inner), *local)
    terms_a = scatter_half(sums_a, 0, 1)
    terms_b = scatter_half(sums_b, 1, 0)
    return pl.pallas_call(
        final_kernel,
        out_shape=jax.ShapeDtypeStruct((512, 512), BF16),
        in_specs=[VMEM] * 10,
        out_specs=VMEM,
        name="result",
    )(mid_a, *terms_a, mid_b, *terms_b)


def solution(mesh):
    placed = (
        P("seq", "wt"),
        P("seq", "wt"),
        P("seq", "wt"),
        P("seq", "wt"),
        P("wt"),
        P(),
        P("wt", None),
        P("wt", None, None, None),
        P("wt", None),
        P("wt", None, None, None),
    )
    return jax.shard_map(
        functools.partial(per_device, mesh.shape["seq"]),
        mesh=mesh,
        in_specs=placed,
        out_specs=P("seq", "wt"),
        check_vma=False,
    )
```

```python
import jax
import jax.numpy as jnp
from jax import lax
from jax.experimental import pallas as pl
from jax.experimental.pallas import tpu as pltpu
from jax.sharding import PartitionSpec as P

HEAD = 128
BLK = 128
SIDE = 4
SEQ = 16
F32 = jnp.float32
BF16 = jnp.bfloat16
VMEM = pl.BlockSpec(memory_space=pltpu.VMEM)
SMEM = pl.BlockSpec(memory_space=pltpu.SMEM)
ANY = pl.BlockSpec(memory_space=pl.ANY)


def feature(a):
    a = a.astype(F32)
    return jnp.where(a > 0, a + 1.0, jnp.exp(jnp.minimum(a, 0.0))).astype(BF16)


def dot(a, b):
    return jnp.dot(a, b, preferred_element_type=F32)


def dot_nt(a, b):
    return lax.dot_general(a, b, (((1,), (1,)), ((), ())), preferred_element_type=F32)


def dot_tn(a, b):
    return lax.dot_general(a, b, (((0,), (0,)), ((), ())), preferred_element_type=F32)


def state_kernel(k_ref, v_ref, out_ref):
    for h in range(4):
        cols = slice(h * HEAD, (h + 1) * HEAD)
        out_ref[h] = dot_tn(feature(k_ref[:, cols]), v_ref[:, cols]).astype(BF16)


def intra_kernel(q_ref, k_ref, v_ref, out_ref):
    half = 256
    row = lax.broadcasted_iota(jnp.int32, (half, half), 0)
    col = lax.broadcasted_iota(jnp.int32, (half, half), 1)
    keep = col <= row
    for h in range(4):
        cols = slice(h * HEAD, (h + 1) * HEAD)
        fq = feature(q_ref[:, cols])
        fk = feature(k_ref[:, cols])
        v = v_ref[:, cols]
        top = jnp.where(keep, dot_nt(fq[:half], fk[:half]), 0.0).astype(BF16)
        out_ref[h, :half] = dot(top, v[:half])
        left = dot_nt(fq[half:], fk[:half]).astype(BF16)
        right = jnp.where(keep, dot_nt(fq[half:], fk[half:]), 0.0).astype(BF16)
        out_ref[h, half:] = dot(left, v[:half]) + dot(right, v[half:])


def mid_kernel(core_ref, q_ref, state_ref, intra_ref, stream_ref, gain_ref, keep_ref, give_ref):
    first = core_ref[0] == 0
    for h in range(4):
        cols = slice(h * HEAD, (h + 1) * HEAD)
        fq = feature(q_ref[:, cols])
        state = state_ref[h]
        high = state.astype(BF16)
        low = (state - high.astype(F32)).astype(BF16)
        raw = intra_ref[h] + dot(fq, high) + dot(fq, low)
        scale = lax.rsqrt(jnp.mean(raw * raw, axis=-1, keepdims=True) + 1e-06)
        attn = raw * scale * gain_ref[:, cols]
        mid = (stream_ref[:, cols].astype(F32) + attn).astype(BF16)
        keep_ref[h] = jnp.where(first, mid[:256], mid[256:])
        give_ref[h] = jnp.where(first, mid[256:], mid[:256])


def ffn_kernel(places_in, places_out, up_index, down_index, gain_ref, *refs):
    pieces, (up_hbm, down_hbm), outs = refs[:8], refs[8:10], refs[10:18]
    x_0, x_1, up_w, down_w, acc_0, acc_1, stage, squares, in_sem, up_sem, down_sem, out_sem = refs[18:]
    xs, accs = (x_0, x_1), (acc_0, acc_1)
    n_hidden, kept = up_w.shape[:2]
    each = 16 // n_hidden

    def piece_copy(i, t):
        source = pieces[i // 2].at[i % 2, t]
        return pltpu.make_async_copy(source, xs[t].at[pl.ds(places_in[i] * 4, 4)], in_sem.at[i, t])

    def up_copy(c):
        return pltpu.make_async_copy(up_hbm.at[c], up_w.at[c], up_sem.at[c])

    def down_copy(c):
        return pltpu.make_async_copy(down_hbm.at[c], down_w.at[c], down_sem.at[c])

    def out_copy(i, t):
        target = outs[i // 2].at[i % 2, t]
        return pltpu.make_async_copy(stage.at[t, pl.ds(i * 4, 4)], target, out_sem.at[i, t])

    def make_ready(i, t):
        total = squares[t]
        for b in range(4):
            block = places_in[i] * 4 + b
            value = xs[t][block].astype(F32)
            total = total + value * value
            xs[t][block] = (value * gain_ref[pl.ds(block, 1), :]).astype(BF16)
        squares[t] = total

    def clear(j, t):
        accs[t][j] = jnp.zeros((256, 128), F32)

    def leave(i, t):
        for b in range(4):
            stage[t, i * 4 + b] = accs[t][places_out[i] * 4 + b].astype(BF16)

    def products(c, t, scale):
        picked = jnp.concatenate([xs[t][up_index[c, k]] for k in range(kept)], axis=1)
        upper = dot(picked, up_w[c].reshape(kept * BLK, BLK)) * scale
        act = (upper / (1.0 + jnp.exp(-upper))).astype(BF16)
        for k in range(0, kept, 2):
            part = dot(act, jnp.concatenate([down_w[c, k], down_w[c, k + 1]], axis=1))
            accs[t][down_index[c, k]] += part[:, :BLK]
            accs[t][down_index[c, k + 1]] += part[:, BLK:]

    def scale_of(t):
        mean = jnp.sum(squares[t], axis=-1, keepdims=True) * (1.0 / (64 * 128))
        return lax.rsqrt(mean + 1e-06)

    for i in range(16):
        piece_copy(i, 0).start()
    for c in range(n_hidden):
        up_copy(c).start()
        down_copy(c).start()
    for i in range(16):
        piece_copy(i, 1).start()
    squares[...] = jnp.zeros(squares.shape, F32)

    @pl.loop(0, 64)
    def _(j):
        clear(j, 0)

    for i in range(16):
        piece_copy(i, 0).wait()
        make_ready(i, 0)
    scale = scale_of(0)

    @pl.loop(0, n_hidden)
    def _(c):
        up_copy(c).wait()
        down_copy(c).wait()
        for e in range(each):
            i = c * each + e
            pltpu.make_async_copy(pieces[0].at[0, 1], x_1.at[pl.ds(0, 4)], in_sem.at[i, 1]).wait()
        for e in range(each):
            i = c * each + e
            make_ready(i, 1)
            for b in range(4):
                clear(i * 4 + b, 1)
        products(c, 0, scale)

    scale_1 = scale_of(1)

    @pl.loop(0, n_hidden)
    def _(c):
        for e in range(each):
            leave(c * each + e, 0)
        products(c, 1, scale_1)
        for i in range(16):

            @pl.when(c == i // each)
            def _():
                out_copy(i, 0).start()

    for i in range(16):
        leave(i, 1)
        out_copy(i, 1).start()
    for i in range(16):
        for t in range(2):
            out_copy(i, t).wait()


PIECE = jax.ShapeDtypeStruct((2, 2, 4, 256, 128), BF16)


def ffn(pieces, places_in, places_out, up_index, down_index, gain, up_blocks, down_blocks):
    n_hidden, kept = up_index.shape
    return pl.pallas_call(
        ffn_kernel,
        out_shape=[PIECE] * 8,
        in_specs=[SMEM] * 4 + [VMEM] + [ANY] * 10,
        out_specs=[ANY] * 8,
        scratch_shapes=[
            pltpu.VMEM((64, 256, 128), BF16),
            pltpu.VMEM((64, 256, 128), BF16),
            pltpu.VMEM((n_hidden, kept, BLK, BLK), BF16),
            pltpu.VMEM((n_hidden, kept, BLK, BLK), BF16),
            pltpu.VMEM((64, 256, 128), F32),
            pltpu.VMEM((64, 256, 128), F32),
            pltpu.VMEM((2, 64, 256, 128), BF16),
            pltpu.VMEM((2, 256, 128), F32),
            pltpu.SemaphoreType.DMA((16, 2)),
            pltpu.SemaphoreType.DMA((n_hidden,)),
            pltpu.SemaphoreType.DMA((n_hidden,)),
            pltpu.SemaphoreType.DMA((16, 2)),
        ],
        name="feed_forward",
        compiler_params=pltpu.CompilerParams(vmem_limit_bytes=52 * 2**20),
        cost_estimate=pl.CostEstimate(
            flops=4 * 512 * n_hidden * kept * BLK * BLK, bytes_accessed=25 * 2**20, transcendentals=512 * 1024
        ),
    )(places_in, places_out, up_index, down_index, gain, *pieces, up_blocks, down_blocks)


def result_kernel(core_ref, mine_ref, traded_ref, out_ref):
    mine = pl.multiple_of(core_ref[0] * 256, 256)
    for b in range(4):
        cols = slice(b * BLK, (b + 1) * BLK)
        out_ref[pl.ds(mine, 256), cols] = mine_ref[b]
        out_ref[pl.ds(256 - mine, 256), cols] = traded_ref[b]


def torus_shift(x, level, step):
    pairs = []
    for s in range(SEQ):
        for a in range(SIDE):
            for b in range(SIDE):
                to = ((a + step) % SIDE, b) if level == s % 2 else (a, (b + step) % SIDE)
                pairs.append(((s * SIDE + a) * SIDE + b, (s * SIDE + to[0]) * SIDE + to[1]))
    return lax.ppermute(x, ("seq", "wt"), pairs)


def swap_cores(x):
    return lax.ppermute(x, "seq", [(s, s ^ 1) for s in range(SEQ)])


def added(*terms):
    total = terms[0].astype(F32)
    for t in terms[1:]:
        total = total + t.astype(F32)
    return total.astype(BF16)


def finished(mid, terms):
    down = terms[0].astype(F32)
    for t in terms[1:]:
        down = down + t.astype(F32)
    return (mid.astype(F32) + down).astype(BF16)


def states_before(own):
    core = lax.axis_index("seq") % 2
    other = swap_cores(own)

    def later(x, places):
        return lax.ppermute(x, "seq", [(s, s + 2 * places) for s in range(SEQ) if s + 2 * places < SEQ])

    both = own.astype(F32) + other.astype(F32)
    pair = jnp.where(core == 0, both[:2], both[2:]).astype(BF16)
    near = later(pair, 1).astype(F32) + later(pair, 2).astype(F32)
    window = (near + pair.astype(F32)).astype(BF16)
    before = near + later(window, 3).astype(F32) + later(window, 6).astype(F32)
    rest = swap_cores(before.astype(BF16)).astype(F32)
    whole = jnp.where(core == 0, jnp.concatenate([before, rest]), jnp.concatenate([rest, before]))
    return whole + jnp.where(core == 0, 0.0, other.astype(F32))


def per_device(queries, keys_in, values_in, stream, attn_gain, mlp_gain, up_index, up_blocks, down_index, down_blocks):
    own = pl.pallas_call(
        state_kernel,
        out_shape=jax.ShapeDtypeStruct((4, HEAD, HEAD), BF16),
        in_specs=[VMEM] * 2,
        out_specs=VMEM,
        name="states",
    )(keys_in, values_in)
    intra = pl.pallas_call(
        intra_kernel,
        out_shape=jax.ShapeDtypeStruct((4, 512, HEAD), F32),
        in_specs=[VMEM] * 3,
        out_specs=VMEM,
        cost_estimate=pl.CostEstimate(flops=2**30, bytes_accessed=3 * 2**20, transcendentals=2**19),
        name="within_block",
    )(queries, keys_in, values_in)
    before = states_before(own)
    half = jax.ShapeDtypeStruct((4, 256, 128), BF16)
    core = lax.axis_index("seq") % 2
    core_arg = core.reshape(1)
    keep, give = pl.pallas_call(
        mid_kernel,
        out_shape=[half, half],
        in_specs=[SMEM] + [VMEM] * 5,
        out_specs=[VMEM] * 2,
        name="mid",
    )(core_arg, queries, before, intra, stream, attn_gain.reshape(1, -1))

    place = lax.axis_index("wt")
    at_x, at_y = place // SIDE, place % SIDE
    number = jnp.arange(16, dtype=jnp.int32)
    outer, inner = jnp.array([0, 1, 3, 2], jnp.int32)[number // 4], number % 4
    step_x, step_y = jnp.where(core == 0, inner, outer), jnp.where(core == 0, outer, inner)

    def where(sign):
        return ((at_x + sign * step_x + SIDE) % SIDE) * SIDE + (at_y + sign * step_y + SIDE) % SIDE

    both = jnp.stack([keep, swap_cores(give)])
    near_1, near_3, near_2 = torus_shift(both, 0, 1), torus_shift(both, 0, -1), torus_shift(both, 0, 2)
    own_a, own_b = jnp.stack([both, near_1]), jnp.stack([near_2, near_3])
    ahead_a = torus_shift(own_a, 1, 1)
    back_b = torus_shift(own_b, 1, -1)
    ahead_b = torus_shift(own_b, 1, 1)
    back_a = torus_shift(own_a, 1, -1)
    far_a = torus_shift(ahead_a, 1, 1)
    far_b = torus_shift(back_b, 1, -1)

    pieces = (own_a, own_b, ahead_a, ahead_b, back_a, back_b, far_a, far_b)
    gain = mlp_gain.reshape(64, BLK)
    own_a, own_b, ahead_a, ahead_b, back_a, back_b, far_a, far_b = ffn(
        pieces, where(-1), where(1), up_index, down_index, gain, up_blocks, down_blocks
    )
    via_a = torus_shift(far_a, 1, 1)
    via_b = torus_shift(far_b, 1, -1)
    from_back_b = torus_shift(ahead_b, 1, 1)
    from_ahead_a = torus_shift(back_a, 1, -1)
    from_back_a = torus_shift(added(via_a, ahead_a), 1, 1)
    from_ahead_b = torus_shift(added(via_b, back_b), 1, -1)
    rows = [added(own_a[r], from_ahead_a[r], from_back_a[r]) for r in range(2)]
    rows += [added(own_b[r], from_ahead_b[r], from_back_b[r]) for r in range(2)]
    terms = [rows[0], torus_shift(rows[1], 0, 1), torus_shift(rows[3], 0, -1), torus_shift(rows[2], 0, 2)]
    done = finished(both, terms)
    return pl.pallas_call(
        result_kernel,
        out_shape=jax.ShapeDtypeStruct((512, 512), BF16),
        in_specs=[SMEM] + [VMEM] * 2,
        out_specs=VMEM,
        name="result",
    )(core_arg, done[0], swap_cores(done[1]))


def solution(mesh):
    placed = (
        P("seq", "wt"),
        P("seq", "wt"),
        P("seq", "wt"),
        P("seq", "wt"),
        P("wt"),
        P(),
        P("wt", None),
        P("wt", None, None, None),
        P("wt", None),
        P("wt", None, None, None),
    )
    return jax.shard_map(
        per_device,
        mesh=mesh,
        in_specs=placed,
        out_specs=P("seq", "wt"),
        check_vma=False,
    )
```

```python
import functools

import jax
import jax.numpy as jnp
from jax import lax
from jax.experimental import pallas as pl
from jax.experimental.pallas import tpu as pltpu
from jax.sharding import PartitionSpec as P

HEAD = 128
BLK = 128
SIDE = 4
SEQ = 16
F32 = jnp.float32
BF16 = jnp.bfloat16
VMEM = pl.BlockSpec(memory_space=pltpu.VMEM)
SMEM = pl.BlockSpec(memory_space=pltpu.SMEM)
ANY = pl.BlockSpec(memory_space=pl.ANY)


def feature(a):
    a = a.astype(F32)
    return jnp.where(a > 0, a + 1.0, jnp.exp(jnp.minimum(a, 0.0))).astype(BF16)


def dot(a, b):
    return jnp.dot(a, b, preferred_element_type=F32)


def dot_nt(a, b):
    return lax.dot_general(a, b, (((1,), (1,)), ((), ())), preferred_element_type=F32)


def dot_tn(a, b):
    return lax.dot_general(a, b, (((0,), (0,)), ((), ())), preferred_element_type=F32)


def state_kernel(k_ref, v_ref, out_ref):
    for h in range(4):
        cols = slice(h * HEAD, (h + 1) * HEAD)
        out_ref[h] = dot_tn(feature(k_ref[:, cols]), v_ref[:, cols]).astype(BF16)


def intra_kernel(q_ref, k_ref, v_ref, out_ref):
    half = 256
    row = lax.broadcasted_iota(jnp.int32, (half, half), 0)
    col = lax.broadcasted_iota(jnp.int32, (half, half), 1)
    keep = col <= row
    for h in range(4):
        cols = slice(h * HEAD, (h + 1) * HEAD)
        fq = feature(q_ref[:, cols])
        fk = feature(k_ref[:, cols])
        v = v_ref[:, cols]
        top = jnp.where(keep, dot_nt(fq[:half], fk[:half]), 0.0).astype(BF16)
        out_ref[h, :half] = dot(top, v[:half])
        left = dot_nt(fq[half:], fk[:half]).astype(BF16)
        right = jnp.where(keep, dot_nt(fq[half:], fk[half:]), 0.0).astype(BF16)
        out_ref[h, half:] = dot(left, v[:half]) + dot(right, v[half:])


def mid_kernel(core_ref, q_ref, state_ref, intra_ref, stream_ref, gain_ref, keep_ref, give_ref):
    first = core_ref[0] == 0
    for h in range(4):
        cols = slice(h * HEAD, (h + 1) * HEAD)
        fq = feature(q_ref[:, cols])
        state = state_ref[h]
        high = state.astype(BF16)
        low = (state - high.astype(F32)).astype(BF16)
        raw = intra_ref[h] + dot(fq, high) + dot(fq, low)
        scale = lax.rsqrt(jnp.mean(raw * raw, axis=-1, keepdims=True) + 1e-06)
        attn = raw * scale * gain_ref[:, cols]
        mid = (stream_ref[:, cols].astype(F32) + attn).astype(BF16)
        keep_ref[h] = jnp.where(first, mid[:256], mid[256:])
        give_ref[h] = jnp.where(first, mid[256:], mid[:256])


def ffn_kernel(t, places_in, places_out, up_index, down_index, gain_ref, *refs):
    pieces, (up_hbm, down_hbm), outs = refs[:8], refs[8:10], refs[10:14]
    x, up_w, down_w, acc, stage, squares, in_sem, up_sem, down_sem, out_sem = refs[14:]
    n_hidden, kept = up_w.shape[:2]

    def piece_copy(i):
        source = pieces[i // 2].at[i % 2 if i >= 12 else 2 * t + i % 2]
        return pltpu.make_async_copy(source, x.at[pl.ds(places_in[i] * 4, 4)], in_sem.at[i])

    def up_copy(c):
        return pltpu.make_async_copy(up_hbm.at[c], up_w.at[c], up_sem.at[c])

    def down_copy(c):
        return pltpu.make_async_copy(down_hbm.at[c], down_w.at[c], down_sem.at[c])

    def out_copy(i):
        return pltpu.make_async_copy(stage.at[pl.ds(i * 4, 4)], outs[i // 4].at[i % 4], out_sem.at[i])

    for i in range(16):
        piece_copy(i).start()
    for c in range(n_hidden):
        up_copy(c).start()
        down_copy(c).start()
    squares[...] = jnp.zeros(squares.shape, F32)

    @pl.loop(0, 64)
    def _(j):
        acc[j] = jnp.zeros((256, 128), F32)

    for i in range(16):
        piece_copy(i).wait()
        total = squares[...]
        for b in range(4):
            block = places_in[i] * 4 + b
            value = x[block].astype(F32)
            total = total + value * value
            x[block] = (value * gain_ref[pl.ds(block, 1), :]).astype(BF16)
        squares[...] = total
    mean = jnp.sum(squares[...], axis=-1, keepdims=True) * (1.0 / (64 * 128))
    scale = lax.rsqrt(mean + 1e-06)

    @pl.loop(0, n_hidden)
    def _(c):
        up_copy(c).wait()
        down_copy(c).wait()
        picked = jnp.concatenate([x[up_index[c, k]] for k in range(kept)], axis=1)
        upper = dot(picked, up_w[c].reshape(kept * BLK, BLK)) * scale
        act = (upper / (1.0 + jnp.exp(-upper))).astype(BF16)
        for k in range(0, kept, 2):
            part = dot(act, jnp.concatenate([down_w[c, k], down_w[c, k + 1]], axis=1))
            acc[down_index[c, k]] += part[:, :BLK]
            acc[down_index[c, k + 1]] += part[:, BLK:]

    for i in range(16):
        for b in range(4):
            stage[i * 4 + b] = acc[places_out[i] * 4 + b].astype(BF16)
        out_copy(i).start()
    for i in range(16):
        out_copy(i).wait()


def ffn(t, pieces, places_in, places_out, up_index, down_index, gain, up_blocks, down_blocks):
    n_hidden, kept = up_index.shape
    return pl.pallas_call(
        functools.partial(ffn_kernel, t),
        out_shape=[jax.ShapeDtypeStruct((4, 4, 256, 128), BF16)] * 4,
        in_specs=[SMEM] * 4 + [VMEM] + [ANY] * 10,
        out_specs=[ANY] * 4,
        scratch_shapes=[
            pltpu.VMEM((64, 256, 128), BF16),
            pltpu.VMEM((n_hidden, kept, BLK, BLK), BF16),
            pltpu.VMEM((n_hidden, kept, BLK, BLK), BF16),
            pltpu.VMEM((64, 256, 128), F32),
            pltpu.VMEM((64, 256, 128), BF16),
            pltpu.VMEM((256, 128), F32),
            pltpu.SemaphoreType.DMA((16,)),
            pltpu.SemaphoreType.DMA((n_hidden,)),
            pltpu.SemaphoreType.DMA((n_hidden,)),
            pltpu.SemaphoreType.DMA((16,)),
        ],
        name="feed_forward",
        compiler_params=pltpu.CompilerParams(vmem_limit_bytes=40 * 2**20),
        cost_estimate=pl.CostEstimate(
            flops=4 * 256 * n_hidden * kept * BLK * BLK, bytes_accessed=17 * 2**20, transcendentals=256 * 1024
        ),
    )(places_in, places_out, up_index, down_index, gain, *pieces, up_blocks, down_blocks)


def result_kernel(core_ref, mine_ref, traded_ref, out_ref):
    mine = pl.multiple_of(core_ref[0] * 256, 256)
    for b in range(4):
        cols = slice(b * BLK, (b + 1) * BLK)
        out_ref[pl.ds(mine, 256), cols] = mine_ref[b]
        out_ref[pl.ds(256 - mine, 256), cols] = traded_ref[b]


def torus_shift(x, level, step):
    pairs = []
    for s in range(SEQ):
        for a in range(SIDE):
            for b in range(SIDE):
                to = ((a + step) % SIDE, b) if level == s % 2 else (a, (b + step) % SIDE)
                pairs.append(((s * SIDE + a) * SIDE + b, (s * SIDE + to[0]) * SIDE + to[1]))
    return lax.ppermute(x, ("seq", "wt"), pairs)


def swap_cores(x):
    return lax.ppermute(x, "seq", [(s, s ^ 1) for s in range(SEQ)])


def by_set(one, two):
    return jnp.stack([one[0], two[0], one[1], two[1]])


def added(*terms):
    total = terms[0].astype(F32)
    for t in terms[1:]:
        total = total + t.astype(F32)
    return total.astype(BF16)


def near_sum(own, ahead, back):
    rows = [added(own[r], ahead[r], back[r]) for r in range(4)]
    return [rows[0], torus_shift(rows[1], 0, 1), torus_shift(rows[3], 0, -1), torus_shift(rows[2], 0, 2)]


def finished(mid, terms):
    down = terms[0].astype(F32)
    for t in terms[1:]:
        down = down + t.astype(F32)
    return (mid.astype(F32) + down).astype(BF16)


def states_before(own):
    core = lax.axis_index("seq") % 2
    other = swap_cores(own)

    def later(x, places):
        return lax.ppermute(x, "seq", [(s, s + 2 * places) for s in range(SEQ) if s + 2 * places < SEQ])

    both = own.astype(F32) + other.astype(F32)
    pair = jnp.where(core == 0, both[:2], both[2:]).astype(BF16)
    near = later(pair, 1).astype(F32) + later(pair, 2).astype(F32)
    window = (near + pair.astype(F32)).astype(BF16)
    before = near + later(window, 3).astype(F32) + later(window, 6).astype(F32)
    rest = swap_cores(before.astype(BF16)).astype(F32)
    whole = jnp.where(core == 0, jnp.concatenate([before, rest]), jnp.concatenate([rest, before]))
    return whole + jnp.where(core == 0, 0.0, other.astype(F32))


def per_device(queries, keys_in, values_in, stream, attn_gain, mlp_gain, up_index, up_blocks, down_index, down_blocks):
    own = pl.pallas_call(
        state_kernel,
        out_shape=jax.ShapeDtypeStruct((4, HEAD, HEAD), BF16),
        in_specs=[VMEM] * 2,
        out_specs=VMEM,
        name="states",
    )(keys_in, values_in)
    intra = pl.pallas_call(
        intra_kernel,
        out_shape=jax.ShapeDtypeStruct((4, 512, HEAD), F32),
        in_specs=[VMEM] * 3,
        out_specs=VMEM,
        cost_estimate=pl.CostEstimate(flops=2**30, bytes_accessed=3 * 2**20, transcendentals=2**19),
        name="within_block",
    )(queries, keys_in, values_in)
    before = states_before(own)
    half = jax.ShapeDtypeStruct((4, 256, 128), BF16)
    core = lax.axis_index("seq") % 2
    core_arg = core.reshape(1)
    keep, give = pl.pallas_call(
        mid_kernel,
        out_shape=[half, half],
        in_specs=[SMEM] + [VMEM] * 5,
        out_specs=[VMEM] * 2,
        name="mid",
    )(core_arg, queries, before, intra, stream, attn_gain.reshape(1, -1))

    place = lax.axis_index("wt")
    at_x, at_y = place // SIDE, place % SIDE
    number = jnp.arange(16, dtype=jnp.int32)
    outer, inner = jnp.array([0, 1, 3, 2], jnp.int32)[number // 4], number % 4
    step_x, step_y = jnp.where(core == 0, inner, outer), jnp.where(core == 0, outer, inner)

    def where(sign):
        return ((at_x + sign * step_x + SIDE) % SIDE) * SIDE + (at_y + sign * step_y + SIDE) % SIDE

    both = jnp.stack([swap_cores(give), keep])
    near_1, near_3, near_2 = torus_shift(both, 0, 1), torus_shift(both, 0, -1), torus_shift(both, 0, 2)
    own_a, own_b = by_set(both, near_1), by_set(near_2, near_3)
    ahead_a = torus_shift(own_a, 1, 1)
    back_b = torus_shift(own_b, 1, -1)
    ahead_b = torus_shift(own_b, 1, 1)
    back_a = torus_shift(own_a, 1, -1)
    far_0 = torus_shift(ahead_a[:2], 1, 1), torus_shift(back_b[:2], 1, -1)
    far_1 = torus_shift(ahead_a[2:], 1, 1), torus_shift(back_b[2:], 1, -1)

    pieces = (own_a, own_b, ahead_a, ahead_b, back_a, back_b)
    gain = mlp_gain.reshape(64, BLK)
    local = (where(-1), where(1), up_index, down_index, gain, up_blocks, down_blocks)

    own_0, ahead_0, back_0, away_0 = ffn(0, (*pieces, *far_0), *local)
    via_0 = torus_shift(away_0, 1, 1)
    from_ahead_0 = torus_shift(back_0, 1, -1)
    far_1, own_0 = lax.optimization_barrier((far_1, own_0))
    own_1, ahead_1, back_1, away_1 = ffn(1, (*pieces, *far_1), *local)
    via_1 = torus_shift(away_1, 1, -1)
    via_0, from_ahead_0, own_1 = lax.optimization_barrier((via_0, from_ahead_0, own_1))
    from_back_0 = torus_shift(added(ahead_0, via_0), 1, 1)
    from_back_1 = torus_shift(ahead_1, 1, 1)
    from_ahead_1 = torus_shift(added(back_1, via_1), 1, -1)
    traded = swap_cores(finished(both[0], near_sum(own_0, from_ahead_0, from_back_0)))
    kept = finished(both[1], near_sum(own_1, from_ahead_1, from_back_1))
    return pl.pallas_call(
        result_kernel,
        out_shape=jax.ShapeDtypeStruct((512, 512), BF16),
        in_specs=[SMEM] + [VMEM] * 2,
        out_specs=VMEM,
        name="result",
    )(core_arg, kept, traded)


def solution(mesh):
    placed = (
        P("seq", "wt"),
        P("seq", "wt"),
        P("seq", "wt"),
        P("seq", "wt"),
        P("wt"),
        P(),
        P("wt", None),
        P("wt", None, None, None),
        P("wt", None),
        P("wt", None, None, None),
    )
    return jax.shard_map(
        per_device,
        mesh=mesh,
        in_specs=placed,
        out_specs=P("seq", "wt"),
        check_vma=False,
    )
```

```python
import functools

import jax
import jax.numpy as jnp
from jax import lax
from jax.experimental import pallas as pl
from jax.experimental.pallas import tpu as pltpu
from jax.sharding import PartitionSpec as P

HEAD = 128
BLK = 128
SIDE = 4
SEQ = 16
F32 = jnp.float32
BF16 = jnp.bfloat16
VMEM = pl.BlockSpec(memory_space=pltpu.VMEM)
SMEM = pl.BlockSpec(memory_space=pltpu.SMEM)
ANY = pl.BlockSpec(memory_space=pl.ANY)


def feature(a):
    a = a.astype(F32)
    return jnp.where(a > 0, a + 1.0, jnp.exp(jnp.minimum(a, 0.0))).astype(BF16)


def dot(a, b):
    return jnp.dot(a, b, preferred_element_type=F32)


def dot_nt(a, b):
    return lax.dot_general(a, b, (((1,), (1,)), ((), ())), preferred_element_type=F32)


def dot_tn(a, b):
    return lax.dot_general(a, b, (((0,), (0,)), ((), ())), preferred_element_type=F32)


def state_kernel(k_ref, v_ref, out_ref):
    for h in range(4):
        cols = slice(h * HEAD, (h + 1) * HEAD)
        out_ref[h] = dot_tn(feature(k_ref[:, cols]), v_ref[:, cols]).astype(BF16)


def intra_kernel(q_ref, k_ref, v_ref, out_ref):
    half = 256
    row = lax.broadcasted_iota(jnp.int32, (half, half), 0)
    col = lax.broadcasted_iota(jnp.int32, (half, half), 1)
    keep = col <= row
    for h in range(4):
        cols = slice(h * HEAD, (h + 1) * HEAD)
        fq = feature(q_ref[:, cols])
        fk = feature(k_ref[:, cols])
        v = v_ref[:, cols]
        top = jnp.where(keep, dot_nt(fq[:half], fk[:half]), 0.0).astype(BF16)
        out_ref[h, :half] = dot(top, v[:half])
        left = dot_nt(fq[half:], fk[:half]).astype(BF16)
        right = jnp.where(keep, dot_nt(fq[half:], fk[half:]), 0.0).astype(BF16)
        out_ref[h, half:] = dot(left, v[:half]) + dot(right, v[half:])


def mid_kernel(core_ref, q_ref, state_ref, intra_ref, stream_ref, gain_ref, keep_ref, give_ref):
    first = core_ref[0] == 0
    for h in range(4):
        cols = slice(h * HEAD, (h + 1) * HEAD)
        fq = feature(q_ref[:, cols])
        state = state_ref[h]
        high = state.astype(BF16)
        low = (state - high.astype(F32)).astype(BF16)
        raw = intra_ref[h] + dot(fq, high) + dot(fq, low)
        scale = lax.rsqrt(jnp.mean(raw * raw, axis=-1, keepdims=True) + 1e-06)
        attn = raw * scale * gain_ref[:, cols]
        mid = (stream_ref[:, cols].astype(F32) + attn).astype(BF16)
        keep_ref[h] = jnp.where(first, mid[:256], mid[256:])
        give_ref[h] = jnp.where(first, mid[256:], mid[:256])


def ffn_kernel(t, places_in, places_out, up_index, down_index, gain_ref, *refs):
    pieces, (up_hbm, down_hbm), outs = refs[:8], refs[8:10], refs[10:14]
    x, up_w, down_w, acc, stage, squares, in_sem, up_sem, down_sem, out_sem = refs[14:]
    n_hidden, kept = up_w.shape[:2]

    def piece_copy(i):
        source = pieces[i // 2].at[i % 2 if i >= 12 else 2 * t + i % 2]
        return pltpu.make_async_copy(source, x.at[pl.ds(places_in[i] * 4, 4)], in_sem.at[i])

    def up_copy(c):
        return pltpu.make_async_copy(up_hbm.at[c], up_w.at[c], up_sem.at[c])

    def down_copy(c):
        return pltpu.make_async_copy(down_hbm.at[c], down_w.at[c], down_sem.at[c])

    def out_copy(i):
        return pltpu.make_async_copy(stage.at[pl.ds(i * 4, 4)], outs[i // 4].at[i % 4], out_sem.at[i])

    for i in range(16):
        piece_copy(i).start()
    squares[...] = jnp.zeros(squares.shape, F32)

    @pl.loop(0, 64)
    def _(j):
        acc[j] = jnp.zeros((256, 128), F32)

    for i in range(16):
        piece_copy(i).wait()
        for c in range(i * n_hidden // 16, (i + 1) * n_hidden // 16):
            up_copy(c).start()
            down_copy(c).start()
        total = squares[...]
        for b in range(4):
            block = places_in[i] * 4 + b
            value = x[block].astype(F32)
            total = total + value * value
            x[block] = (value * gain_ref[pl.ds(block, 1), :]).astype(BF16)
        squares[...] = total
    mean = jnp.sum(squares[...], axis=-1, keepdims=True) * (1.0 / (64 * 128))
    scale = lax.rsqrt(mean + 1e-06)

    @pl.loop(0, n_hidden)
    def _(c):
        up_copy(c).wait()
        down_copy(c).wait()
        picked = jnp.concatenate([x[up_index[c, k]] for k in range(kept)], axis=1)
        upper = dot(picked, up_w[c].reshape(kept * BLK, BLK)) * scale
        act = (upper / (1.0 + jnp.exp(-upper))).astype(BF16)
        for k in range(0, kept, 2):
            part = dot(act, jnp.concatenate([down_w[c, k], down_w[c, k + 1]], axis=1))
            acc[down_index[c, k]] += part[:, :BLK]
            acc[down_index[c, k + 1]] += part[:, BLK:]

    for i in range(16):
        for b in range(4):
            stage[i * 4 + b] = acc[places_out[i] * 4 + b].astype(BF16)
        out_copy(i).start()
    for i in range(16):
        out_copy(i).wait()


def ffn(t, pieces, places_in, places_out, up_index, down_index, gain, up_blocks, down_blocks):
    n_hidden, kept = up_index.shape
    return pl.pallas_call(
        functools.partial(ffn_kernel, t),
        out_shape=[jax.ShapeDtypeStruct((4, 4, 256, 128), BF16)] * 4,
        in_specs=[SMEM] * 4 + [VMEM] + [ANY] * 10,
        out_specs=[ANY] * 4,
        scratch_shapes=[
            pltpu.VMEM((64, 256, 128), BF16),
            pltpu.VMEM((n_hidden, kept, BLK, BLK), BF16),
            pltpu.VMEM((n_hidden, kept, BLK, BLK), BF16),
            pltpu.VMEM((64, 256, 128), F32),
            pltpu.VMEM((64, 256, 128), BF16),
            pltpu.VMEM((256, 128), F32),
            pltpu.SemaphoreType.DMA((16,)),
            pltpu.SemaphoreType.DMA((n_hidden,)),
            pltpu.SemaphoreType.DMA((n_hidden,)),
            pltpu.SemaphoreType.DMA((16,)),
        ],
        name="feed_forward",
        compiler_params=pltpu.CompilerParams(vmem_limit_bytes=40 * 2**20),
        cost_estimate=pl.CostEstimate(
            flops=4 * 256 * n_hidden * kept * BLK * BLK, bytes_accessed=17 * 2**20, transcendentals=256 * 1024
        ),
    )(places_in, places_out, up_index, down_index, gain, *pieces, up_blocks, down_blocks)


def result_kernel(core_ref, mine_ref, traded_ref, out_ref):
    mine = pl.multiple_of(core_ref[0] * 256, 256)
    for b in range(4):
        cols = slice(b * BLK, (b + 1) * BLK)
        out_ref[pl.ds(mine, 256), cols] = mine_ref[b]
        out_ref[pl.ds(256 - mine, 256), cols] = traded_ref[b]


def torus_shift(x, level, step):
    pairs = []
    for s in range(SEQ):
        for a in range(SIDE):
            for b in range(SIDE):
                to = ((a + step) % SIDE, b) if level == s % 2 else (a, (b + step) % SIDE)
                pairs.append(((s * SIDE + a) * SIDE + b, (s * SIDE + to[0]) * SIDE + to[1]))
    return lax.ppermute(x, ("seq", "wt"), pairs)


def swap_cores(x):
    return lax.ppermute(x, "seq", [(s, s ^ 1) for s in range(SEQ)])


def by_set(one, two):
    return jnp.stack([one[0], two[0], one[1], two[1]])


def added(*terms):
    total = terms[0].astype(F32)
    for t in terms[1:]:
        total = total + t.astype(F32)
    return total.astype(BF16)


def near_sum(own, ahead, back):
    rows = [added(own[r], ahead[r], back[r]) for r in range(4)]
    return [rows[0], torus_shift(rows[1], 0, 1), torus_shift(rows[3], 0, -1), torus_shift(rows[2], 0, 2)]


def finished(mid, terms):
    down = terms[0].astype(F32)
    for t in terms[1:]:
        down = down + t.astype(F32)
    return (mid.astype(F32) + down).astype(BF16)


def states_before(own, beside):
    core = lax.axis_index("seq") % 2
    other = swap_cores(own)

    def later(x, places):
        return lax.ppermute(x, "seq", [(s, s + 2 * places) for s in range(SEQ) if s + 2 * places < SEQ])

    both = own.astype(F32) + other.astype(F32)
    pair = jnp.where(core == 0, both[:2], both[2:]).astype(BF16)
    near = later(pair, 1).astype(F32) + later(pair, 2).astype(F32)
    near, beside = lax.optimization_barrier((near, beside))
    window = (near + pair.astype(F32)).astype(BF16)
    before = near + later(window, 3).astype(F32) + later(window, 6).astype(F32)
    rest = swap_cores(before.astype(BF16)).astype(F32)
    whole = jnp.where(core == 0, jnp.concatenate([before, rest]), jnp.concatenate([rest, before]))
    return whole + jnp.where(core == 0, 0.0, other.astype(F32)), beside


def per_device(queries, keys_in, values_in, stream, attn_gain, mlp_gain, up_index, up_blocks, down_index, down_blocks):
    own = pl.pallas_call(
        state_kernel,
        out_shape=jax.ShapeDtypeStruct((4, HEAD, HEAD), BF16),
        in_specs=[VMEM] * 2,
        out_specs=VMEM,
        name="states",
    )(keys_in, values_in)
    intra = pl.pallas_call(
        intra_kernel,
        out_shape=jax.ShapeDtypeStruct((4, 512, HEAD), F32),
        in_specs=[VMEM] * 3,
        out_specs=VMEM,
        cost_estimate=pl.CostEstimate(flops=2**30, bytes_accessed=3 * 2**20, transcendentals=2**19),
        name="within_block",
    )(queries, keys_in, values_in)
    before, intra = states_before(own, intra)
    half = jax.ShapeDtypeStruct((4, 256, 128), BF16)
    core = lax.axis_index("seq") % 2
    core_arg = core.reshape(1)
    keep, give = pl.pallas_call(
        mid_kernel,
        out_shape=[half, half],
        in_specs=[SMEM] + [VMEM] * 5,
        out_specs=[VMEM] * 2,
        name="mid",
    )(core_arg, queries, before, intra, stream, attn_gain.reshape(1, -1))

    place = lax.axis_index("wt")
    at_x, at_y = place // SIDE, place % SIDE
    number = jnp.arange(16, dtype=jnp.int32)
    outer, inner = jnp.array([0, 1, 3, 2], jnp.int32)[number // 4], number % 4
    step_x, step_y = jnp.where(core == 0, inner, outer), jnp.where(core == 0, outer, inner)

    def where(sign):
        return ((at_x + sign * step_x + SIDE) % SIDE) * SIDE + (at_y + sign * step_y + SIDE) % SIDE

    both = jnp.stack([swap_cores(give), keep])
    near_1, near_3, near_2 = torus_shift(both, 0, 1), torus_shift(both, 0, -1), torus_shift(both, 0, 2)
    own_a, own_b = by_set(both, near_1), by_set(near_2, near_3)
    ahead_a = torus_shift(own_a, 1, 1)
    back_b = torus_shift(own_b, 1, -1)
    ahead_b = torus_shift(own_b, 1, 1)
    back_a = torus_shift(own_a, 1, -1)
    far_0 = torus_shift(ahead_a[:2], 1, 1), torus_shift(back_b[:2], 1, -1)
    far_1 = torus_shift(ahead_a[2:], 1, 1), torus_shift(back_b[2:], 1, -1)

    pieces = (own_a, own_b, ahead_a, ahead_b, back_a, back_b)
    gain = mlp_gain.reshape(64, BLK)
    local = (where(-1), where(1), up_index, down_index, gain, up_blocks, down_blocks)

    own_0, ahead_0, back_0, away_0 = ffn(0, (*pieces, *far_0), *local)
    via_0 = torus_shift(away_0, 1, 1)
    from_ahead_0 = torus_shift(back_0, 1, -1)
    far_1, own_0 = lax.optimization_barrier((far_1, own_0))
    own_1, ahead_1, back_1, away_1 = ffn(1, (*pieces, *far_1), *local)
    via_1 = torus_shift(away_1, 1, -1)
    via_0, from_ahead_0, own_1 = lax.optimization_barrier((via_0, from_ahead_0, own_1))
    from_back_0 = torus_shift(added(ahead_0, via_0), 1, 1)
    from_back_1 = torus_shift(ahead_1, 1, 1)
    from_ahead_1 = torus_shift(added(back_1, via_1), 1, -1)
    traded = swap_cores(finished(both[0], near_sum(own_0, from_ahead_0, from_back_0)))
    kept = finished(both[1], near_sum(own_1, from_ahead_1, from_back_1))
    return pl.pallas_call(
        result_kernel,
        out_shape=jax.ShapeDtypeStruct((512, 512), BF16),
        in_specs=[SMEM] + [VMEM] * 2,
        out_specs=VMEM,
        name="result",
    )(core_arg, kept, traded)


def solution(mesh):
    placed = (
        P("seq", "wt"),
        P("seq", "wt"),
        P("seq", "wt"),
        P("seq", "wt"),
        P("wt"),
        P(),
        P("wt", None),
        P("wt", None, None, None),
        P("wt", None),
        P("wt", None, None, None),
    )
    return jax.shard_map(
        per_device,
        mesh=mesh,
        in_specs=placed,
        out_specs=P("seq", "wt"),
        check_vma=False,
    )
```

```python
import functools

import jax
import jax.numpy as jnp
from jax import lax
from jax.experimental import pallas as pl
from jax.experimental.pallas import tpu as pltpu
from jax.sharding import PartitionSpec as P

HEAD = 128
BLK = 128
SIDE = 4
SEQ = 16
F32 = jnp.float32
BF16 = jnp.bfloat16
VMEM = pl.BlockSpec(memory_space=pltpu.VMEM)
SMEM = pl.BlockSpec(memory_space=pltpu.SMEM)
ANY = pl.BlockSpec(memory_space=pl.ANY)


def feature(a):
    a = a.astype(F32)
    return jnp.where(a > 0, a + 1.0, jnp.exp(jnp.minimum(a, 0.0))).astype(BF16)


def dot(a, b):
    return jnp.dot(a, b, preferred_element_type=F32)


def dot_nt(a, b):
    return lax.dot_general(a, b, (((1,), (1,)), ((), ())), preferred_element_type=F32)


def dot_tn(a, b):
    return lax.dot_general(a, b, (((0,), (0,)), ((), ())), preferred_element_type=F32)


def state_kernel(k_ref, v_ref, out_ref):
    for h in range(4):
        cols = slice(h * HEAD, (h + 1) * HEAD)
        out_ref[h] = dot_tn(feature(k_ref[:, cols]), v_ref[:, cols]).astype(BF16)


def intra_kernel(q_ref, k_ref, v_ref, out_ref):
    half = 256
    row = lax.broadcasted_iota(jnp.int32, (half, half), 0)
    col = lax.broadcasted_iota(jnp.int32, (half, half), 1)
    keep = col <= row
    for h in range(4):
        cols = slice(h * HEAD, (h + 1) * HEAD)
        fq = feature(q_ref[:, cols])
        fk = feature(k_ref[:, cols])
        v = v_ref[:, cols]
        top = jnp.where(keep, dot_nt(fq[:half], fk[:half]), 0.0).astype(BF16)
        out_ref[h, :half] = dot(top, v[:half])
        left = dot_nt(fq[half:], fk[:half]).astype(BF16)
        right = jnp.where(keep, dot_nt(fq[half:], fk[half:]), 0.0).astype(BF16)
        out_ref[h, half:] = dot(left, v[:half]) + dot(right, v[half:])


def mid_kernel(core_ref, q_ref, state_ref, intra_ref, stream_ref, gain_ref, keep_ref, give_ref):
    first = core_ref[0] == 0
    for h in range(4):
        cols = slice(h * HEAD, (h + 1) * HEAD)
        fq = feature(q_ref[:, cols])
        state = state_ref[h]
        high = state.astype(BF16)
        low = (state - high.astype(F32)).astype(BF16)
        raw = intra_ref[h] + dot(fq, high) + dot(fq, low)
        scale = lax.rsqrt(jnp.mean(raw * raw, axis=-1, keepdims=True) + 1e-06)
        attn = raw * scale * gain_ref[:, cols]
        mid = (stream_ref[:, cols].astype(F32) + attn).astype(BF16)
        keep_ref[h] = jnp.where(first, mid[:256], mid[256:])
        give_ref[h] = jnp.where(first, mid[256:], mid[:256])


def ffn_kernel(t, places_in, places_out, up_index, down_index, gain_ref, *refs):
    pieces, (up_hbm, down_hbm), outs = refs[:8], refs[8:10], refs[10:14]
    x, up_w, down_w, acc, stage, squares, act, in_sem, up_sem, down_sem, out_sem = refs[14:]
    n_hidden, kept = up_w.shape[:2]

    def piece_copy(i):
        source = pieces[i // 2].at[i % 2 if i >= 12 else 2 * t + i % 2]
        return pltpu.make_async_copy(source, x.at[pl.ds(places_in[i] * 4, 4)], in_sem.at[i])

    def up_copy(c):
        return pltpu.make_async_copy(up_hbm.at[c], up_w.at[c], up_sem.at[c])

    def down_copy(c):
        return pltpu.make_async_copy(down_hbm.at[c], down_w.at[c], down_sem.at[c])

    def out_copy(i):
        return pltpu.make_async_copy(stage.at[pl.ds(i * 4, 4)], outs[i // 4].at[i % 4], out_sem.at[i])

    for i in range(16):
        piece_copy(i).start()
    squares[...] = jnp.zeros(squares.shape, F32)

    @pl.loop(0, 64)
    def _(j):
        acc[j] = jnp.zeros((256, 128), F32)

    for i in range(16):
        piece_copy(i).wait()
        for c in range(i * n_hidden // 16, (i + 1) * n_hidden // 16):
            up_copy(c).start()
            down_copy(c).start()
        total = squares[...]
        for b in range(4):
            block = places_in[i] * 4 + b
            value = x[block].astype(F32)
            total = total + value * value
            x[block] = (value * gain_ref[pl.ds(block, 1), :]).astype(BF16)
        squares[...] = total
    mean = jnp.sum(squares[...], axis=-1, keepdims=True) * (1.0 / (64 * 128))
    scale = lax.rsqrt(mean + 1e-06)

    def activated(c):
        picked = jnp.concatenate([x[up_index[c, k]] for k in range(kept)], axis=1)
        upper = dot(picked, up_w[c].reshape(kept * BLK, BLK)) * scale
        return (upper / (1.0 + jnp.exp(-upper))).astype(BF16)

    def spread(c, units):
        for k in range(kept):
            acc[down_index[c, k]] += dot(units, down_w[c, k])

    up_copy(0).wait()
    act[...] = activated(0)

    @pl.loop(0, n_hidden - 1)
    def _(c):
        down_copy(c).wait()
        up_copy(c + 1).wait()
        units = act[...]
        spread(c, units)
        act[...] = activated(c + 1)

    down_copy(n_hidden - 1).wait()
    spread(n_hidden - 1, act[...])

    for i in range(16):
        for b in range(4):
            stage[i * 4 + b] = acc[places_out[i] * 4 + b].astype(BF16)
        out_copy(i).start()
    for i in range(16):
        out_copy(i).wait()


def ffn(t, pieces, places_in, places_out, up_index, down_index, gain, up_blocks, down_blocks):
    n_hidden, kept = up_index.shape
    return pl.pallas_call(
        functools.partial(ffn_kernel, t),
        out_shape=[jax.ShapeDtypeStruct((4, 4, 256, 128), BF16)] * 4,
        in_specs=[SMEM] * 4 + [VMEM] + [ANY] * 10,
        out_specs=[ANY] * 4,
        scratch_shapes=[
            pltpu.VMEM((64, 256, 128), BF16),
            pltpu.VMEM((n_hidden, kept, BLK, BLK), BF16),
            pltpu.VMEM((n_hidden, kept, BLK, BLK), BF16),
            pltpu.VMEM((64, 256, 128), F32),
            pltpu.VMEM((64, 256, 128), BF16),
            pltpu.VMEM((256, 128), F32),
            pltpu.VMEM((256, 128), BF16),
            pltpu.SemaphoreType.DMA((16,)),
            pltpu.SemaphoreType.DMA((n_hidden,)),
            pltpu.SemaphoreType.DMA((n_hidden,)),
            pltpu.SemaphoreType.DMA((16,)),
        ],
        name="feed_forward",
        compiler_params=pltpu.CompilerParams(vmem_limit_bytes=40 * 2**20),
        cost_estimate=pl.CostEstimate(
            flops=4 * 256 * n_hidden * kept * BLK * BLK, bytes_accessed=17 * 2**20, transcendentals=256 * 1024
        ),
    )(places_in, places_out, up_index, down_index, gain, *pieces, up_blocks, down_blocks)


def result_kernel(core_ref, mine_ref, traded_ref, out_ref):
    mine = pl.multiple_of(core_ref[0] * 256, 256)
    for b in range(4):
        cols = slice(b * BLK, (b + 1) * BLK)
        out_ref[pl.ds(mine, 256), cols] = mine_ref[b]
        out_ref[pl.ds(256 - mine, 256), cols] = traded_ref[b]


def torus_shift(x, level, step):
    pairs = []
    for s in range(SEQ):
        for a in range(SIDE):
            for b in range(SIDE):
                to = ((a + step) % SIDE, b) if level == s % 2 else (a, (b + step) % SIDE)
                pairs.append(((s * SIDE + a) * SIDE + b, (s * SIDE + to[0]) * SIDE + to[1]))
    return lax.ppermute(x, ("seq", "wt"), pairs)


def swap_cores(x):
    return lax.ppermute(x, "seq", [(s, s ^ 1) for s in range(SEQ)])


def by_set(one, two):
    return jnp.stack([one[0], two[0], one[1], two[1]])


def added(*terms):
    total = terms[0].astype(F32)
    for t in terms[1:]:
        total = total + t.astype(F32)
    return total.astype(BF16)


def near_sum(own, ahead, back):
    rows = [added(own[r], ahead[r], back[r]) for r in range(4)]
    return [rows[0], torus_shift(rows[1], 0, 1), torus_shift(rows[3], 0, -1), torus_shift(rows[2], 0, 2)]


def finished(mid, terms):
    down = terms[0].astype(F32)
    for t in terms[1:]:
        down = down + t.astype(F32)
    return (mid.astype(F32) + down).astype(BF16)


def states_before(own, beside):
    core = lax.axis_index("seq") % 2
    other = swap_cores(own)

    def later(x, places):
        return lax.ppermute(x, "seq", [(s, s + 2 * places) for s in range(SEQ) if s + 2 * places < SEQ])

    both = own.astype(F32) + other.astype(F32)
    pair = jnp.where(core == 0, both[:2], both[2:]).astype(BF16)
    near = later(pair, 1).astype(F32) + later(pair, 2).astype(F32)
    near, beside = lax.optimization_barrier((near, beside))
    window = (near + pair.astype(F32)).astype(BF16)
    before = near + later(window, 3).astype(F32) + later(window, 6).astype(F32)
    rest = swap_cores(before.astype(BF16)).astype(F32)
    whole = jnp.where(core == 0, jnp.concatenate([before, rest]), jnp.concatenate([rest, before]))
    return whole + jnp.where(core == 0, 0.0, other.astype(F32)), beside


def per_device(queries, keys_in, values_in, stream, attn_gain, mlp_gain, up_index, up_blocks, down_index, down_blocks):
    own = pl.pallas_call(
        state_kernel,
        out_shape=jax.ShapeDtypeStruct((4, HEAD, HEAD), BF16),
        in_specs=[VMEM] * 2,
        out_specs=VMEM,
        name="states",
    )(keys_in, values_in)
    intra = pl.pallas_call(
        intra_kernel,
        out_shape=jax.ShapeDtypeStruct((4, 512, HEAD), F32),
        in_specs=[VMEM] * 3,
        out_specs=VMEM,
        cost_estimate=pl.CostEstimate(flops=2**30, bytes_accessed=3 * 2**20, transcendentals=2**19),
        name="within_block",
    )(queries, keys_in, values_in)
    before, intra = states_before(own, intra)
    half = jax.ShapeDtypeStruct((4, 256, 128), BF16)
    core = lax.axis_index("seq") % 2
    core_arg = core.reshape(1)
    keep, give = pl.pallas_call(
        mid_kernel,
        out_shape=[half, half],
        in_specs=[SMEM] + [VMEM] * 5,
        out_specs=[VMEM] * 2,
        name="mid",
    )(core_arg, queries, before, intra, stream, attn_gain.reshape(1, -1))

    place = lax.axis_index("wt")
    at_x, at_y = place // SIDE, place % SIDE
    number = jnp.arange(16, dtype=jnp.int32)
    outer, inner = jnp.array([0, 1, 3, 2], jnp.int32)[number // 4], number % 4
    step_x, step_y = jnp.where(core == 0, inner, outer), jnp.where(core == 0, outer, inner)

    def where(sign):
        return ((at_x + sign * step_x + SIDE) % SIDE) * SIDE + (at_y + sign * step_y + SIDE) % SIDE

    both = jnp.stack([swap_cores(give), keep])
    near_1, near_3, near_2 = torus_shift(both, 0, 1), torus_shift(both, 0, -1), torus_shift(both, 0, 2)
    own_a, own_b = by_set(both, near_1), by_set(near_2, near_3)
    ahead_a = torus_shift(own_a, 1, 1)
    back_b = torus_shift(own_b, 1, -1)
    ahead_b = torus_shift(own_b, 1, 1)
    back_a = torus_shift(own_a, 1, -1)
    far_0 = torus_shift(ahead_a[:2], 1, 1), torus_shift(back_b[:2], 1, -1)
    far_1 = torus_shift(ahead_a[2:], 1, 1), torus_shift(back_b[2:], 1, -1)

    pieces = (own_a, own_b, ahead_a, ahead_b, back_a, back_b)
    gain = mlp_gain.reshape(64, BLK)
    local = (where(-1), where(1), up_index, down_index, gain, up_blocks, down_blocks)

    own_0, ahead_0, back_0, away_0 = ffn(0, (*pieces, *far_0), *local)
    via_0 = torus_shift(away_0, 1, 1)
    from_ahead_0 = torus_shift(back_0, 1, -1)
    far_1, own_0 = lax.optimization_barrier((far_1, own_0))
    own_1, ahead_1, back_1, away_1 = ffn(1, (*pieces, *far_1), *local)
    via_1 = torus_shift(away_1, 1, -1)
    via_0, from_ahead_0, own_1 = lax.optimization_barrier((via_0, from_ahead_0, own_1))
    from_back_0 = torus_shift(added(ahead_0, via_0), 1, 1)
    from_back_1 = torus_shift(ahead_1, 1, 1)
    from_ahead_1 = torus_shift(added(back_1, via_1), 1, -1)
    traded = swap_cores(finished(both[0], near_sum(own_0, from_ahead_0, from_back_0)))
    kept = finished(both[1], near_sum(own_1, from_ahead_1, from_back_1))
    return pl.pallas_call(
        result_kernel,
        out_shape=jax.ShapeDtypeStruct((512, 512), BF16),
        in_specs=[SMEM] + [VMEM] * 2,
        out_specs=VMEM,
        name="result",
    )(core_arg, kept, traded)


def solution(mesh):
    placed = (
        P("seq", "wt"),
        P("seq", "wt"),
        P("seq", "wt"),
        P("seq", "wt"),
        P("wt"),
        P(),
        P("wt", None),
        P("wt", None, None, None),
        P("wt", None),
        P("wt", None, None, None),
    )
    return jax.shard_map(
        per_device,
        mesh=mesh,
        in_specs=placed,
        out_specs=P("seq", "wt"),
        check_vma=False,
    )
```
